256 devices in a mesh: dp: 32 (over y, x, core), mp: 8 (over z).
Axes of the slice: x: 4, y: 4, z: 8, core: 2. Of those that a mesh axis runs over, the one named last changes fastest.
Arguments:
- inputs: bfloat16 [16384, 6144], P('dp', 'mp'), may hold values from -13 to 13, as said below
- out_grad: bfloat16 [16384, 3072], P('dp', 'mp'), may hold values from -6 to 6
- weight: bfloat16 [6144, 3072], P('dp', 'mp'), may hold values from -2 to 2, as said below
- momentum: float32 [6144, 3072], P('dp', 'mp'), may hold values from -6 to 6
- variance: float32 [6144, 3072], P('dp', 'mp'), may hold values from 0.25 to 4
- server_error: float32 [6144, 3072], P('dp', 'mp'), may hold values from -4 to 4
- worker_error: bfloat16 [32, 6144, 3072], P('dp', None, 'mp'), may hold values from -1.5 to 1.5
Outputs:
- input_grad: bfloat16 [16384, 6144], P('dp', 'mp')
- momentum_next: float32 [6144, 3072], P('dp', 'mp')
- server_next: float32 [6144, 3072], P('dp', 'mp')
- worker_next: bfloat16 [32, 6144, 3072], P('dp', None, 'mp')
- refreshed: bfloat16 [16384, 3072], P('dp', 'mp')
The draws below stay inside these ranges and needn't reach their ends.
Inputs may be any that keep to these rules, and one draw needn't show every extreme that they name: `inputs`: activations whose features have different scales. `weight`: A projection whose rows have different scales.
All inputs are finite; a program needn't handle non-finite values. Where the reference program divides by a largest or mean magnitude, that divisor is 1e-20 or more.
Results may differ from the reference program's by a relative error of at most 0.009.
Values may be sent and summed in bfloat16 or wider, within the bound.
No kernel may reach another device: no remote copies, remote signals or barrier semaphores. Data moves between devices by JAX's collectives and lax.ppermute only.
A program may use at most 128 MiB of HBM per device.

```python
import math
import jax
import jax.numpy as jnp
from jax import lax

D = 6144
TOK_DEV = 512
QW = 3072
TOKENS = 16384
N_DP = 32
N_MP = 8


def draw_inputs(key, part):
    key = jax.random.fold_in(key, 11)
    first, second = jax.random.split(key)
    spread = jax.random.uniform(second, (1, D), jnp.float32)
    base = jnp.clip(jax.random.normal(first, (TOKENS, D), jnp.float32), -4.0, 4.0)
    scales = jnp.exp(2.3 * spread - 1.15)
    return (base * scales).astype(jnp.bfloat16)


def draw_weight(key, part):
    key = jax.random.fold_in(key, 23)
    first, second = jax.random.split(key)
    position = jnp.arange(D, dtype=jnp.float32)[:, None] / D
    rise = 0.6 + 1.2 * position
    spread = jnp.exp(2.3 * (jax.random.uniform(second, (D, 1), jnp.float32) - 0.5))
    base = jnp.clip(jax.random.normal(first, (D, QW), jnp.float32), -3.0, 3.0)
    return (base * rise * spread / jnp.sqrt(jnp.float32(D))).astype(jnp.bfloat16)


def steps_of(key, shape, pieces, least, high):
    def one(axis_at, shards_of):
        draws = jax.random.uniform(jax.random.fold_in(jax.random.fold_in(key, 6), axis_at), (shards_of,), jnp.float32, least / len(pieces), high / len(pieces))
        return jnp.repeat(jnp.exp(draws), shape[axis_at] // shards_of).reshape((-1,) + (1,) * (len(shape) - axis_at - 1))

    gain = one(*pieces[0])
    for cut in pieces[1:]:
        gain = gain * one(*cut)
    return gain


def centred(stream_key, extent, deviation, reach, cuts=(), kind=jnp.bfloat16):
    entries = jax.random.normal(stream_key, extent, jnp.float32) * deviation
    if len(cuts) > 0:
        entries = steps_of(stream_key, extent, cuts, -0.22, 0.18) * entries
    return jnp.clip(entries, min=-reach, max=reach).astype(kind)


def setup_inputs(seed: int = 0) -> dict:
    key_of = jax.random.split(jax.random.key(seed), 8)
    return {
        "inputs": draw_inputs(jax.random.fold_in(key_of[7], 71), 0),
        "out_grad": centred(key_of[1], (TOKENS, QW), 1.0, 6.0, ((0, 32), (1, 8))),
        "weight": draw_weight(jax.random.fold_in(key_of[7], 71), 0),
        "momentum": centred(key_of[3], (D, QW), 1.0, 6.0, ((0, 32), (1, 8)), jnp.float32),
        "variance": jnp.clip(jnp.exp(math.log(4.0) - 2.7725887 * jax.random.uniform(key_of[4], (D, QW), jnp.float32) ** steps_of(key_of[4], (D, QW), ((0, 32), (1, 8)), -0.2, 0.2)), 0.25, 4.0),
        "server_error": centred(key_of[5], (D, QW), 0.3, 4.0, ((0, 32), (1, 8)), jnp.float32),
        "worker_error": centred(key_of[6], (N_DP, D, QW), 0.1, 1.5, ((0, 32), (2, 8))),
    }


def squash(values, rows, cols):
    total_rows, total_cols = values.shape
    blocks = values.reshape(total_rows // rows, rows, total_cols // cols, cols)
    level = lax.optimization_barrier(jnp.mean(jnp.abs(blocks), axis=(1, 3), keepdims=True)) + 1e-06
    return (level * jnp.tanh(blocks / level)).reshape(total_rows, total_cols)

def reference(inputs, out_grad, weight, momentum, variance, server_error, worker_error):
    rows = D // N_DP
    cols = QW // N_MP
    factor = 1.0 / math.sqrt(TOKENS)
    input_grad = jnp.dot(out_grad, weight.T, preferred_element_type=jnp.float32).astype(jnp.bfloat16)
    token_sets = inputs.reshape(N_DP, TOK_DEV, D)
    grad_sets = out_grad.reshape(N_DP, TOK_DEV, QW)

    def worker(total, items):
        tokens_i, grads_i, error_i = items
        partial_value = lax.dot_general(tokens_i, grads_i, (((0,), (0,)), ((), ())), preferred_element_type=jnp.float32) * factor
        corrected = partial_value + error_i.astype(jnp.float32)
        packed = squash(corrected, rows, cols).astype(jnp.bfloat16)
        error_next = (corrected - packed.astype(jnp.float32)).astype(jnp.bfloat16)
        return (total + packed.astype(jnp.float32), error_next)
    gradient, worker_next = lax.scan(worker, jnp.zeros((D, QW), jnp.float32), (token_sets, grad_sets, worker_error))
    momentum_next = 0.9 * momentum + 0.1 * gradient
    held = momentum_next + server_error
    squeezed = squash(held, rows, cols)
    server_next = held - squeezed
    direction = (squeezed / (jnp.sqrt(variance) + 1e-06)).astype(jnp.bfloat16)
    weight_sq = jnp.sum(jnp.square(weight.astype(jnp.float32)))
    step_sq = jnp.sum(jnp.square(direction.astype(jnp.float32)))
    ratio = jnp.sqrt(weight_sq / (step_sq + 1e-12))
    new_weight = (weight.astype(jnp.float32) - 0.25 * ratio * direction.astype(jnp.float32)).astype(jnp.bfloat16)
    refreshed = jnp.dot(inputs, new_weight, preferred_element_type=jnp.float32).astype(jnp.bfloat16)
    return (input_grad, momentum_next, server_next, worker_next, refreshed)
```

```python
import functools
import math

import jax
import jax.numpy as jnp
from jax import lax
from jax.experimental import pallas as pl
from jax.experimental.pallas import tpu as pltpu
from jax.sharding import PartitionSpec as P

BF = jnp.bfloat16
F32 = jnp.float32
NY, NX, NC, NZ = 4, 4, 2, 8
VMEM_LIMIT = 48 * 1024 * 1024


def flat_dp(y, x, c):
    return (y * NX + x) * NC + c


def coords(d):
    return d // (NX * NC), (d // NC) % NX, d % NC


def x_shift(r):
    return [(d, flat_dp(y, (x + r) % NX, c)) for d in range(32) for y, x, c in [coords(d)]]


def y_shift(r):
    return [(d, flat_dp((y + r) % NY, x, c)) for d in range(32) for y, x, c in [coords(d)]]


def xor_perm(n, bit):
    return [(i, i ^ bit) for i in range(n)]


NEAR = [(z, z ^ 1) for z in range(NZ)]
FAR = [(z, (z - 1) % NZ if z % 2 == 0 else (z + 1) % NZ) for z in range(NZ)]


def params():
    return pltpu.CompilerParams(vmem_limit_bytes=VMEM_LIMIT)


def shard_body(halves, fresh_next, fresh_pair, factor, sc, *refs):
    n_a = 2 if halves else 1
    a_refs = refs[:n_a]
    og_ref, we_ref = refs[n_a], refs[n_a + 1]
    skip = (0 if fresh_next else 1) + (0 if fresh_pair else 2)
    wn_ref, keep_ref, send_ref = refs[n_a + 2 + skip :]
    half = pl.program_id(0)
    if halves:
        a = jnp.where(half == 0, a_refs[0][...], a_refs[1][...])
    else:
        a = a_refs[0][...]
    partial = lax.dot_general(a, og_ref[...], (((0,), (0,)), ((), ())), preferred_element_type=F32)
    corrected = partial * factor + we_ref[0].astype(F32)
    rows = corrected.shape[0] // 2
    out = []
    for b in range(2):
        block = corrected[b * rows : (b + 1) * rows]
        level = jnp.sum(jnp.abs(block), axis=(0, 1), keepdims=True) * (1.0 / block.size) + 1e-06
        packed = (level * jnp.tanh(block / level)).astype(BF)
        wn_ref[0, b * rows : (b + 1) * rows] = (block - packed.astype(F32)).astype(BF)
        out.append(packed)
    first = sc[1] == 0
    keep_ref[0] = jnp.where(first, out[0], out[1])
    send_ref[0] = jnp.where(first, out[1], out[0])


def shard_grad(parts, og, worker_error, m, core, slot, wn, pair, factor):
    tokens, cols = og.shape
    wide = worker_error.shape[1] // NZ // 2
    halves = len(parts) == 2
    fresh_next, fresh_pair = wn is None, pair is None
    in_specs = (
        [pl.BlockSpec((tokens, wide), lambda h, s: (0, 0))] * 2
        if halves
        else [pl.BlockSpec((tokens, wide), lambda h, s: (0, h))]
    )
    in_specs += [
        pl.BlockSpec((tokens, cols), lambda h, s: (0, 0)),
        pl.BlockSpec((1, wide, cols), lambda h, s: (0, 2 * s[0] + h, 0)),
    ]
    args = list(parts) + [og, worker_error]
    aliases = {}
    if not fresh_next:
        aliases[1 + len(args)] = 0
        args.append(wn)
        in_specs.append(pl.BlockSpec(memory_space=pl.ANY))
    if not fresh_pair:
        for k in range(2):
            aliases[1 + len(args)] = 1 + k
            args.append(pair[k])
            in_specs.append(pl.BlockSpec(memory_space=pl.ANY))
    out = pl.pallas_call(
        functools.partial(shard_body, halves, fresh_next, fresh_pair, factor),
        grid_spec=pltpu.PrefetchScalarGridSpec(
            num_scalar_prefetch=1,
            grid=(2,),
            in_specs=in_specs,
            out_specs=[
                pl.BlockSpec((1, wide, cols), lambda h, s: (0, 2 * s[0] + h, 0)),
                pl.BlockSpec((1, wide // 2, cols), lambda h, s: (2 * slot + h, 0, 0)),
                pl.BlockSpec((1, wide // 2, cols), lambda h, s: (2 * slot + h, 0, 0)),
            ],
        ),
        out_shape=[
            jax.ShapeDtypeStruct(worker_error.shape, BF),
            jax.ShapeDtypeStruct((4, wide // 2, cols), BF),
            jax.ShapeDtypeStruct((4, wide // 2, cols), BF),
        ],
        input_output_aliases=aliases,
        compiler_params=params(),
        cost_estimate=pl.CostEstimate(
            flops=2 * tokens * 2 * wide * cols, bytes_accessed=4 * 2 * wide * cols * 2, transcendentals=0
        ),
        name="shard_grad",
    )(jnp.stack([m, core]).astype(jnp.int32), *args)
    return out[0], (out[1], out[2])


def core_sum_body(sc, keep_ref, recv_ref, *outs):
    for r in range(NX):
        x = lax.rem(sc[0] + r, NX)
        at = jnp.bitwise_xor(x // 2, sc[1]) * 2 + lax.rem(x, 2)
        outs[r][...] = (keep_ref[at].astype(F32) + recv_ref[at].astype(F32)).astype(BF)


def core_sum(keep, recv, x, parity):
    whole = pl.BlockSpec(keep.shape, lambda i, s: (0, 0, 0))
    one = pl.BlockSpec(keep.shape[1:], lambda i, s: (0, 0))
    return pl.pallas_call(
        core_sum_body,
        grid_spec=pltpu.PrefetchScalarGridSpec(
            num_scalar_prefetch=1, grid=(1,), in_specs=[whole] * 2, out_specs=[one] * 4
        ),
        out_shape=[jax.ShapeDtypeStruct(keep.shape[1:], BF)] * 4,
        compiler_params=params(),
        cost_estimate=pl.CostEstimate(flops=keep.size, bytes_accessed=6 * keep.size, transcendentals=0),
        name="core_sum",
    )(jnp.stack([x, parity]).astype(jnp.int32), keep, recv)


def x_sum_body(sc, a, b, c, d, *rest):
    rest[-1][0] = (
        a[...].astype(F32) + b[...].astype(F32) + c[...].astype(F32) + d[...].astype(F32)
    ).astype(BF)


def x_sum(blocks, slot, held):
    shape = blocks[0].shape
    one = pl.BlockSpec(shape, lambda i, s: (0, 0))
    args = list(blocks)
    in_specs = [one] * 4
    aliases = {}
    if held is not None:
        aliases[1 + len(args)] = 0
        args.append(held)
        in_specs = in_specs + [pl.BlockSpec(memory_space=pl.ANY)]
    return pl.pallas_call(
        x_sum_body,
        grid_spec=pltpu.PrefetchScalarGridSpec(
            num_scalar_prefetch=1,
            grid=(1,),
            in_specs=in_specs,
            out_specs=pl.BlockSpec((1,) + shape, lambda i, s: (s[0], 0, 0)),
        ),
        out_shape=jax.ShapeDtypeStruct((4,) + shape, BF),
        input_output_aliases=aliases,
        compiler_params=params(),
        name="x_sum",
    )(slot[None].astype(jnp.int32), *args)


def update_body(g0, g1, g2, g3, w, mom, var, err, mom_out, err_out, dir_out, sums):
    gradient = (
        g0[0].astype(F32) + g1[...].astype(F32) + g2[...].astype(F32) + g3[...].astype(F32)
    )
    momentum = 0.9 * mom[...] + 0.1 * gradient
    mom_out[...] = momentum
    held = momentum + err[...]
    level = jnp.sum(jnp.abs(held), axis=(0, 1), keepdims=True) * (1.0 / held.size) + 1e-06
    squeezed = level * jnp.tanh(held / level)
    err_out[...] = held - squeezed
    direction = (squeezed / (jnp.sqrt(var[...]) + 1e-06)).astype(BF)
    dir_out[...] = direction
    wf = w[...].astype(F32)
    df = direction.astype(F32)
    total_w = jnp.sum(wf * wf, axis=(0, 1), keepdims=True)
    total_d = jnp.sum(df * df, axis=(0, 1), keepdims=True)
    row = lax.broadcasted_iota(jnp.int32, sums.shape, 0)
    sums[...] = jnp.where(row == 0, total_w, total_d)


def update(xr, got, weight, momentum, variance, server_error):
    shape = weight.shape
    one = pl.BlockSpec(shape, lambda i: (0, 0))
    return pl.pallas_call(
        update_body,
        grid=(1,),
        in_specs=[pl.BlockSpec((1,) + shape, lambda i: (0, 0, 0))] + [one] * 7,
        out_specs=[one, one, one, pl.BlockSpec((8, 128), lambda i: (0, 0))],
        out_shape=[
            jax.ShapeDtypeStruct(shape, F32),
            jax.ShapeDtypeStruct(shape, F32),
            jax.ShapeDtypeStruct(shape, BF),
            jax.ShapeDtypeStruct((8, 128), F32),
        ],
        compiler_params=params(),
        name="update",
    )(xr, *got, weight, momentum, variance, server_error)


def product(sc, shards_in, b_ref):
    total = None
    for k, a in enumerate(shards_in):
        part = jnp.dot(a, b_ref[sc[k]], preferred_element_type=F32)
        total = part if total is None else total + part
    return total


def forward_body(sc, *refs):
    b_ref, out = refs[9], refs[10]
    mats = [r[...] for r in refs[:7]] + [jnp.concatenate([refs[7][...], refs[8][...]], axis=1)]
    out[...] = product(sc, mats, b_ref)


def forward_end_body(sc, *refs):
    b_ref, base, scale, out = refs[9:]
    mats = [r[...] for r in refs[:7]] + [jnp.concatenate([refs[7][...], refs[8][...]], axis=1)]
    out[...] = (base[...] - scale[...] * product(sc, mats, b_ref)).astype(BF)


def forward(parts, ms, matrix, base=None, scale=None):
    tokens = parts[0].shape[0]
    cols = matrix.shape[-1]
    blocks = matrix.reshape(NZ, -1, cols)
    args = list(parts) + [blocks] + ([] if base is None else [base, scale])
    in_specs = [pl.BlockSpec(v.shape, lambda i, s, n=v.ndim: (0,) * n) for v in args]
    return pl.pallas_call(
        forward_body if base is None else forward_end_body,
        grid_spec=pltpu.PrefetchScalarGridSpec(
            num_scalar_prefetch=1,
            grid=(1,),
            in_specs=in_specs,
            out_specs=pl.BlockSpec((tokens, cols), lambda i, s: (0, 0)),
        ),
        out_shape=jax.ShapeDtypeStruct((tokens, cols), F32 if base is None else BF),
        compiler_params=params(),
        cost_estimate=pl.CostEstimate(
            flops=2 * tokens * cols * matrix.size // cols, bytes_accessed=2 * matrix.size * 3, transcendentals=0
        ),
        name="forward",
    )(jnp.stack(ms).astype(jnp.int32), *args)


def input_grad_body(og, w, out, acc):
    j = pl.program_id(0)
    part = lax.dot_general(og[0], w[0], (((1,), (1,)), ((), ())), preferred_element_type=F32)

    @pl.when(j == 0)
    def _():
        acc[...] = part

    @pl.when(j > 0)
    def _():
        acc[...] += part

    @pl.when(j == NZ - 1)
    def _():
        out[...] = acc[...].astype(BF)


def input_grad_of(og_all, rows):
    _, tokens, cols = og_all.shape
    width = rows.shape[1]
    return pl.pallas_call(
        input_grad_body,
        grid=(NZ,),
        in_specs=[
            pl.BlockSpec((1, tokens, cols), lambda j: (j, 0, 0)),
            pl.BlockSpec((1, width, cols), lambda j: (j, 0, 0)),
        ],
        out_specs=pl.BlockSpec((tokens, width), lambda j: (0, 0)),
        out_shape=jax.ShapeDtypeStruct((tokens, width), BF),
        scratch_shapes=[pltpu.VMEM((tokens, width), F32)],
        compiler_params=params(),
        cost_estimate=pl.CostEstimate(
            flops=2 * NZ * tokens * cols * width, bytes_accessed=2 * (og_all.size + rows.size), transcendentals=0
        ),
        name="input_grad",
    )(og_all, rows)


def shards(inputs, out_grad, weight, momentum, variance, server_error, worker_error):
    groups = lax.axis_size("dp")
    factor = 1.0 / math.sqrt(inputs.shape[0] * groups)
    rows, cols = weight.shape
    z = lax.axis_index("mp")
    d = lax.axis_index("dp")
    y, x, core = d // (NX * NC), (d // NC) % NX, d % NC
    parity = z % 2
    sign = 1 - 2 * parity
    wide = inputs.shape[1] // 2

    columns = lax.all_gather(weight, "dp", axis=0, tiled=True)
    perm = [
        (dp * NZ + mp, (4 * mp + dp % 4) * NZ + dp // 4) for dp in range(32) for mp in range(NZ)
    ]
    moved = lax.ppermute(weight, ("dp", "mp"), perm)
    plane = lax.all_gather(moved, "dp", axis=0, tiled=True).reshape(NZ, 4 * rows, cols)

    def near(a):
        return lax.ppermute(a, "mp", NEAR)

    def away(a):
        return lax.ppermute(a, "mp", FAR)

    u1, v1 = near(inputs), away(inputs)
    u2, v2 = near(v1), away(u1)
    u3, v3 = near(v2), away(u2)
    f0, f1 = near(v3[:, :wide]), away(u3[:, wide:])

    def at(k):
        return lax.rem(z + k * sign + 2 * NZ, NZ)

    order = [(inputs,), (u1,), (v2,), (v1,), (u2,), (u3,), (f0, f1), (v3,)]
    ms = [at(0), at(1), at(-2), at(-1), at(2), at(3), at(4), at(-3)]
    sequence = [(0, 1), (3, 2), (4, 5), (7, 6)]
    wn, held = None, None
    for p, pair_of in enumerate(sequence):
        pair = None
        for k in pair_of:
            wn, pair = shard_grad(
                order[k], out_grad, worker_error, ms[k], core, k % 2, wn, pair, factor
            )
        keep, send = pair
        recv = lax.ppermute(send, "dp", xor_perm(32, 1))
        mine = core_sum(keep, recv, x, parity)
        blocks = [mine[0]] + [lax.ppermute(mine[r], "dp", x_shift(r)) for r in (1, 2, 3)]
        owner = ms[2 * p] // 2
        held = x_sum(blocks, lax.rem(owner - y + NY, NY), held)
    got = [lax.ppermute(held[r], "dp", y_shift(r)) for r in (1, 2, 3)]
    momentum_next, server_next, direction, sums = update(
        held, got, weight, momentum, variance, server_error
    )
    directions = lax.all_gather(direction, "dp", axis=0, tiled=True)
    for axis, n, bit in (
        ("dp", 32, 1),
        ("dp", 32, 2),
        ("dp", 32, 4),
        ("dp", 32, 8),
        ("dp", 32, 16),
        ("mp", NZ, 1),
        ("mp", NZ, 2),
        ("mp", NZ, 4),
    ):
        sums = sums + lax.ppermute(sums, axis, xor_perm(n, bit))
    ratio = jnp.sqrt(sums[0:1, 0:1] / (sums[1:2, 0:1] + 1e-12))

    later = out_grad + (f0[0, 0] * 0 + f1[0, 0] * 0)
    og_all = lax.all_gather(later, "mp", axis=0, tiled=False)
    input_grad = input_grad_of(og_all, plane)

    parts = [inputs, u1, v2, v1, u2, u3, v3, f0, f1]
    slots = ms[:6] + [ms[7], ms[6]]
    base = forward(parts, slots, columns)
    refreshed = forward(parts, slots, directions, base, 0.25 * ratio)
    return (input_grad, momentum_next, server_next, wn, refreshed)


def solution(mesh):
    return jax.shard_map(
        shards,
        mesh=mesh,
        in_specs=(
            P("dp", "mp"),
            P("dp", "mp"),
            P("dp", "mp"),
            P("dp", "mp"),
            P("dp", "mp"),
            P("dp", "mp"),
            P("dp", None, "mp"),
        ),
        out_specs=(P("dp", "mp"), P("dp", "mp"), P("dp", "mp"), P("dp", None, "mp"), P("dp", "mp")),
        check_vma=False,
    )
```

```python
import functools
import math

import jax
import jax.numpy as jnp
from jax import lax
from jax.experimental import pallas as pl
from jax.experimental.pallas import tpu as pltpu
from jax.sharding import PartitionSpec as P

BF = jnp.bfloat16
F32 = jnp.float32
NY, NX, NC, NZ = 4, 4, 2, 8
MIB = 1024 * 1024


def flat_dp(y, x, c):
    return (y * NX + x) * NC + c


def coords(d):
    return d // (NX * NC), (d // NC) % NX, d % NC


def x_shift(r):
    return [(d, flat_dp(y, (x + r) % NX, c)) for d in range(32) for y, x, c in [coords(d)]]


def y_shift(r):
    return [(d, flat_dp((y + r) % NY, x, c)) for d in range(32) for y, x, c in [coords(d)]]


def xor_perm(n, bit):
    return [(i, i ^ bit) for i in range(n)]


NEAR = [(z, z ^ 1) for z in range(NZ)]
FAR = [(z, (z - 1) % NZ if z % 2 == 0 else (z + 1) % NZ) for z in range(NZ)]


def params(mib=60):
    return pltpu.CompilerParams(vmem_limit_bytes=mib * MIB)


CORE, X, PARITY, SLOT = 8, 9, 10, 11


def shard_body(n_parts, ks, fresh, factor, sc, *refs):
    at = 0
    step = pl.program_id(0)
    values = []
    for n in n_parts:
        if n == 2:
            values.append(jnp.where(step % 2 == 0, refs[at][...], refs[at + 1][...]))
        else:
            values.append(refs[at][...])
        at += n
    og_ref, we_ref = refs[at], refs[at + 1]
    wn_ref, keep_ref, send_ref = refs[at + (2 if fresh else 3) :]
    a = values[0] if len(values) == 1 else jnp.where(step < 2, values[0], values[1])
    partial = lax.dot_general(a, og_ref[...], (((0,), (0,)), ((), ())), preferred_element_type=F32)
    corrected = partial * factor + we_ref[0].astype(F32)
    rows = corrected.shape[0] // 2
    out = []
    for b in range(2):
        block = corrected[b * rows : (b + 1) * rows]
        level = jnp.sum(jnp.abs(block), axis=(0, 1), keepdims=True) * (1.0 / block.size) + 1e-06
        packed = (level * jnp.tanh(block / level)).astype(BF)
        wn_ref[0, b * rows : (b + 1) * rows] = (block - packed.astype(F32)).astype(BF)
        out.append(packed)
    first = sc[CORE] == 0
    keep_ref[0] = jnp.where(first, out[0], out[1])
    send_ref[0] = jnp.where(first, out[1], out[0])


def shard_grad(sc, parts, ks, og, worker_error, wn, factor):
    tokens, cols = og.shape
    wide = worker_error.shape[1] // NZ // 2
    count = 2 * len(parts)
    in_specs, args = [], []
    for k, part in enumerate(parts):
        for piece in part:
            if len(part) == 2:
                in_specs.append(pl.BlockSpec((tokens, wide), lambda g, s: (0, 0)))
            else:
                in_specs.append(
                    pl.BlockSpec(
                        (tokens, wide), lambda g, s, k=k: (0, jnp.clip(g - 2 * k, 0, 1))
                    )
                )
            args.append(piece)

    def error_at(g, s):
        m = s[ks[0]] if len(ks) == 1 else jnp.where(g < 2, s[ks[0]], s[ks[1]])
        return (0, 2 * m + g % 2, 0)

    in_specs += [
        pl.BlockSpec((tokens, cols), lambda g, s: (0, 0)),
        pl.BlockSpec((1, wide, cols), error_at),
    ]
    args += [og, worker_error]
    aliases = {}
    if wn is not None:
        aliases[1 + len(args)] = 0
        args.append(wn)
        in_specs.append(pl.BlockSpec(memory_space=pl.ANY))
    block = pl.BlockSpec((1, wide // 2, cols), lambda g, s: (g, 0, 0))
    half = jax.ShapeDtypeStruct((count, wide // 2, cols), BF)
    return pl.pallas_call(
        functools.partial(shard_body, [len(p) for p in parts], ks, wn is None, factor),
        grid_spec=pltpu.PrefetchScalarGridSpec(
            num_scalar_prefetch=1,
            grid=(count,),
            in_specs=in_specs,
            out_specs=[pl.BlockSpec((1, wide, cols), error_at), block, block],
        ),
        out_shape=[jax.ShapeDtypeStruct(worker_error.shape, BF), half, half],
        input_output_aliases=aliases,
        compiler_params=params(),
        cost_estimate=pl.CostEstimate(
            flops=2 * tokens * count * wide * cols,
            bytes_accessed=6 * count * wide * cols,
            transcendentals=0,
        ),
        name="shard_grad",
    )(sc, *args)


def core_sum_body(n, sc, *refs):
    outs = refs[4 * n :]
    for r in range(NX):
        x = lax.rem(sc[X] + r, NX)
        same = jnp.bitwise_xor(x // 2, sc[PARITY]) == 0
        h = lax.rem(x, 2)
        for p in range(n):
            a, ra, b, rb = refs[4 * p : 4 * p + 4]
            first = a[h].astype(F32) + ra[h].astype(F32)
            second = b[h].astype(F32) + rb[h].astype(F32)
            outs[r][p] = jnp.where(same, first, second).astype(outs[r].dtype)


def core_sum(sc, pairs):
    tail = pairs[0][0][0].shape[1:]
    n = len(pairs)
    args, in_specs = [], []
    for pair in pairs:
        for keep, recv, half in pair:
            args += [keep, recv]
            in_specs += [pl.BlockSpec((2,) + tail, lambda i, s, half=half: (half, 0, 0))] * 2
    one = pl.BlockSpec((n,) + tail, lambda i, s: (0, 0, 0))
    return pl.pallas_call(
        functools.partial(core_sum_body, n),
        grid_spec=pltpu.PrefetchScalarGridSpec(
            num_scalar_prefetch=1, grid=(1,), in_specs=in_specs, out_specs=[one] * 4
        ),
        out_shape=[jax.ShapeDtypeStruct((n,) + tail, F32 if r == 0 else BF) for r in range(NX)],
        compiler_params=params(),
        name="core_sum",
    )(sc, *args)


def x_sum_body(counts, sc, *refs):
    outs, held = refs[-5:-1], refs[-1]
    at, p = 0, 0
    for n in counts:
        for k in range(n):
            held[sc[SLOT + p]] = sum(refs[at + r][k].astype(F32) for r in range(NX))
            p += 1
        at += NX
    for r in range(NY):
        outs[r][...] = held[r].astype(outs[r].dtype)


def x_sum(sc, groups):
    tail = groups[0][0].shape[1:]
    args = [v for group in groups for v in group]
    one = pl.BlockSpec(tail, lambda i, s: (0, 0))
    return pl.pallas_call(
        functools.partial(x_sum_body, [g[0].shape[0] for g in groups]),
        grid_spec=pltpu.PrefetchScalarGridSpec(
            num_scalar_prefetch=1,
            grid=(1,),
            in_specs=[pl.BlockSpec(v.shape, lambda i, s: (0, 0, 0)) for v in args],
            out_specs=[one] * 4,
            scratch_shapes=[pltpu.VMEM((NY,) + tail, F32)],
        ),
        out_shape=[jax.ShapeDtypeStruct(tail, F32 if r == 0 else BF) for r in range(NY)],
        compiler_params=params(),
        name="x_sum",
    )(sc, *args)


def update_body(g0, g1, g2, g3, w, mom, var, err, mom_out, err_out, dir_out, sums):
    gradient = (
        g0[...] + g1[...].astype(F32) + g2[...].astype(F32) + g3[...].astype(F32)
    )
    momentum = 0.9 * mom[...] + 0.1 * gradient
    mom_out[...] = momentum
    held = momentum + err[...]
    level = jnp.sum(jnp.abs(held), axis=(0, 1), keepdims=True) * (1.0 / held.size) + 1e-06
    squeezed = level * jnp.tanh(held / level)
    err_out[...] = held - squeezed
    direction = (squeezed / (jnp.sqrt(var[...]) + 1e-06)).astype(BF)
    dir_out[...] = direction
    wf = w[...].astype(F32)
    df = direction.astype(F32)
    total_w = jnp.sum(wf * wf, axis=(0, 1), keepdims=True)
    total_d = jnp.sum(df * df, axis=(0, 1), keepdims=True)
    row = lax.broadcasted_iota(jnp.int32, sums.shape, 0)
    sums[...] = jnp.where(row == 0, total_w, total_d)


def update(mine, got, weight, momentum, variance, server_error):
    shape = weight.shape
    one = pl.BlockSpec(shape, lambda i: (0, 0))
    return pl.pallas_call(
        update_body,
        grid=(1,),
        in_specs=[one] * 8,
        out_specs=[one, one, one, pl.BlockSpec((8, 128), lambda i: (0, 0))],
        out_shape=[
            jax.ShapeDtypeStruct(shape, F32),
            jax.ShapeDtypeStruct(shape, F32),
            jax.ShapeDtypeStruct(shape, BF),
            jax.ShapeDtypeStruct((8, 128), F32),
        ],
        compiler_params=params(),
        name="update",
    )(mine, *got, weight, momentum, variance, server_error)


def forward_body(n_parts, ending, sc, *refs):
    n = sum(n_parts)
    pieces, b_hbm = refs[:n], refs[n]
    base = refs[n + 1 : n + 3] if ending else ()
    out, a_held, b_held, a_sems, b_sems = refs[-5:]
    rows = b_held.shape[1]
    waits = []
    at = 0
    for k, parts in enumerate(n_parts):
        wide = rows // parts
        mine = []
        for j in range(parts):
            target = a_held.at[k] if parts == 1 else a_held.at[k, :, j * wide : (j + 1) * wide]
            mine.append(pltpu.make_async_copy(pieces[at], target, a_sems.at[at]))
            at += 1
        if len(b_hbm.shape) == 5:
            for i in range(4):
                target = b_held.at[k, i * (rows // 4) : (i + 1) * (rows // 4)]
                mine.append(pltpu.make_async_copy(b_hbm.at[sc[k], i, 0], target, b_sems.at[k]))
        else:
            mine.append(pltpu.make_async_copy(b_hbm.at[sc[k]], b_held.at[k], b_sems.at[k]))
        for copy in mine:
            copy.start()
        waits.append(mine)
    total = None
    for k, mine in enumerate(waits):
        for copy in mine:
            copy.wait()
        part = jnp.dot(a_held[k], b_held[k], preferred_element_type=F32)
        total = part if total is None else total + part
    if ending:
        total = base[0][...] - base[1][0:1, 0:1] * total
    out[...] = total.astype(out.dtype)


def forward(sc, parts, matrix, base=None, scale=None):
    tokens = parts[0][0].shape[0]
    rows, cols = parts[0][0].shape[1], matrix.shape[-1]
    args = [v for part in parts for v in part]
    n = len(args)
    args = args + [matrix]
    in_specs = [pl.BlockSpec(memory_space=pl.ANY)] * (n + 1)
    if base is not None:
        args += [base, scale]
        in_specs += [
            pl.BlockSpec((tokens, cols), lambda i, s: (0, 0)),
            pl.BlockSpec(scale.shape, lambda i, s: (0, 0)),
        ]
    return pl.pallas_call(
        functools.partial(forward_body, [len(p) for p in parts], base is not None),
        grid_spec=pltpu.PrefetchScalarGridSpec(
            num_scalar_prefetch=1,
            grid=(1,),
            in_specs=in_specs,
            out_specs=pl.BlockSpec((tokens, cols), lambda i, s: (0, 0)),
            scratch_shapes=[
                pltpu.VMEM((NZ, tokens, rows), BF),
                pltpu.VMEM((NZ, rows, cols), BF),
                pltpu.SemaphoreType.DMA((n,)),
                pltpu.SemaphoreType.DMA((NZ,)),
            ],
        ),
        out_shape=jax.ShapeDtypeStruct((tokens, cols), F32 if base is None else BF),
        compiler_params=params(),
        cost_estimate=pl.CostEstimate(
            flops=2 * NZ * tokens * cols * rows, bytes_accessed=2 * matrix.size * 3, transcendentals=0
        ),
        name="forward",
    )(sc, *args)


def input_grad_body(sc, og, w, out, acc):
    j = pl.program_id(0)
    wide = jnp.concatenate([w[0, i, 0] for i in range(4)])
    part = lax.dot_general(og[0], wide, (((1,), (1,)), ((), ())), preferred_element_type=F32)

    @pl.when(j == 0)
    def _():
        acc[...] = part

    @pl.when(j > 0)
    def _():
        acc[...] += part

    @pl.when(j == NZ - 1)
    def _():
        out[...] = acc[...].astype(BF)


def input_grad_of(sc, og_all, both):
    _, tokens, cols = og_all.shape
    width = 4 * both.shape[3]
    return pl.pallas_call(
        input_grad_body,
        grid_spec=pltpu.PrefetchScalarGridSpec(
            num_scalar_prefetch=1,
            grid=(NZ,),
            in_specs=[
                pl.BlockSpec((1, tokens, cols), lambda j, s: (lax.rem(j - s[0] + NZ, NZ), 0, 0)),
                pl.BlockSpec((1, 4, 1, width // 4, cols), lambda j, s: (j, 0, 1, 0, 0)),
            ],
            out_specs=pl.BlockSpec((tokens, width), lambda j, s: (0, 0)),
            scratch_shapes=[pltpu.VMEM((tokens, width), F32)],
        ),
        out_shape=jax.ShapeDtypeStruct((tokens, width), BF),
        compiler_params=params(),
        cost_estimate=pl.CostEstimate(
            flops=2 * NZ * tokens * cols * width, bytes_accessed=2 * og_all.size, transcendentals=0
        ),
        name="input_grad",
    )(sc, og_all, both)


def shards(inputs, out_grad, weight, momentum, variance, server_error, worker_error):
    groups = lax.axis_size("dp")
    factor = 1.0 / math.sqrt(inputs.shape[0] * groups)
    rows, cols = weight.shape
    z = lax.axis_index("mp")
    d = lax.axis_index("dp")
    y, x, core = d // (NX * NC), (d // NC) % NX, d % NC
    parity = z % 2
    sign = 1 - 2 * parity
    wide = inputs.shape[1] // 2

    spread_perm, along_perm = [], []
    for dp in range(32):
        yy, xx, cc = coords(dp)
        for zz in range(NZ):
            row = 2 * yy + xx // 2
            place = (row + zz) % NZ
            to = flat_dp(place // 2, 2 * (place % 2) + xx % 2, cc)
            spread_perm.append((dp * NZ + zz, to * NZ + zz))
            along_perm.append((to * NZ + zz, to * NZ + row))

    def near(a):
        return lax.ppermute(a, "mp", NEAR)

    def away(a):
        return lax.ppermute(a, "mp", FAR)

    def at(k):
        return lax.rem(z + k * sign + 2 * NZ, NZ)

    ms = [at(0), at(1), at(-1), at(-2), at(2), at(3), at(-3), at(4)]
    slots = [lax.rem(ms[k] // 2 - y + NY, NY) for k in (0, 3, 4, 7)]
    sc = jnp.stack(ms + [core, x, parity] + slots).astype(jnp.int32)
    tie = lax.optimization_barrier

    def grad(parts, ks, wn):
        return shard_grad(sc, parts, ks, out_grad, worker_error, wn, factor)

    def swap(send):
        return lax.ppermute(send, "dp", xor_perm(32, 1))

    def spread(mine):
        return [mine[0]] + [lax.ppermute(mine[r], "dp", x_shift(r)) for r in (1, 2, 3)]

    moved = lax.ppermute(weight, ("dp", "mp"), spread_perm)
    moved = lax.ppermute(moved, ("dp", "mp"), along_perm)
    u1, v1 = near(inputs), away(inputs)
    u1, v1, moved = tie((u1, v1, moved))

    both = lax.all_gather(jnp.concatenate([weight, moved]), "dp", axis=0, tiled=True)
    both = both.reshape(NZ, 4, 2, rows, cols)
    u2, v2 = near(v1), away(u1)
    wn, keep0, send0 = grad([(inputs,)], [0], None)
    recv0 = swap(send0)
    wn, keep1, send1 = grad([(u1,), (v1,)], [1, 2], wn)
    recv1 = swap(send1)
    u2, v2, wn, recv0, recv1 = tie((u2, v2, wn, recv0, recv1))

    u3, v3 = near(v2), away(u2)
    wn, keep2, send2 = grad([(v2,), (u2,)], [3, 4], wn)
    recv2 = swap(send2)
    sums01 = core_sum(
        sc,
        [
            ((keep0, recv0, 0), (keep1, recv1, 0)),
            ((keep2, recv2, 0), (keep1, recv1, 1)),
        ],
    )
    u3, v3, wn, sums01 = tie((u3, v3, wn, sums01))

    g0, g1, wn = tie((v3[:, :wide], u3[:, wide:], wn))
    f0, f1 = near(g0), away(g1)
    wn, keep3, send3 = grad([(u3,), (v3,)], [5, 6], wn)
    f0, f1, wn, send3, later = tie((f0, f1, wn, send3, out_grad))

    og_all = lax.all_gather(later, "mp", axis=0, tiled=False)
    blocks01 = spread(sums01)
    recv3 = swap(send3)
    wn, keep4, send4 = grad([(f0, f1)], [7], wn)
    recv4 = swap(send4)
    sums23 = core_sum(
        sc,
        [
            ((keep2, recv2, 1), (keep3, recv3, 0)),
            ((keep4, recv4, 0), (keep3, recv3, 1)),
        ],
    )
    blocks23 = spread(sums23)
    parts = [(inputs,), (u1,), (v1,), (v2,), (u2,), (u3,), (v3,), (f0, f1)]
    base = forward(sc, parts, both)
    blocks23, base = tie((blocks23, base))
    by_y = x_sum(sc, [blocks01, blocks23])
    got = [lax.ppermute(by_y[r], "dp", y_shift(r)) for r in (1, 2, 3)]
    momentum_next, server_next, direction, sums = update(
        by_y[0], got, weight, momentum, variance, server_error
    )
    directions = lax.all_gather(direction, "dp", axis=0, tiled=True)
    for axis, n, bit in (
        ("dp", 32, 1),
        ("dp", 32, 2),
        ("dp", 32, 4),
        ("dp", 32, 8),
        ("dp", 32, 16),
        ("mp", NZ, 1),
        ("mp", NZ, 2),
        ("mp", NZ, 4),
    ):
        sums = sums + lax.ppermute(sums, axis, xor_perm(n, bit))
    ratio = jnp.sqrt(sums[0:1] / (sums[1:2] + 1e-12))

    input_grad = input_grad_of(sc, og_all, both)

    refreshed = forward(sc, parts, directions.reshape(NZ, 4 * rows, cols), base, 0.25 * ratio)
    return (input_grad, momentum_next, server_next, wn, refreshed)


def solution(mesh):
    return jax.shard_map(
        shards,
        mesh=mesh,
        in_specs=(
            P("dp", "mp"),
            P("dp", "mp"),
            P("dp", "mp"),
            P("dp", "mp"),
            P("dp", "mp"),
            P("dp", "mp"),
            P("dp", None, "mp"),
        ),
        out_specs=(P("dp", "mp"), P("dp", "mp"), P("dp", "mp"), P("dp", None, "mp"), P("dp", "mp")),
        check_vma=False,
    )
```

```python
import functools
import math

import jax
import jax.numpy as jnp
from jax import lax
from jax.experimental import pallas as pl
from jax.experimental.pallas import tpu as pltpu
from jax.sharding import PartitionSpec as P

BF = jnp.bfloat16
F32 = jnp.float32
NY, NX, NC, NZ = 4, 4, 2, 8
MIB = 1024 * 1024


def flat_dp(y, x, c):
    return (y * NX + x) * NC + c


def coords(d):
    return d // (NX * NC), (d // NC) % NX, d % NC


def x_shift(r):
    return [(d, flat_dp(y, (x + r) % NX, c)) for d in range(32) for y, x, c in [coords(d)]]


def y_shift(r):
    return [(d, flat_dp((y + r) % NY, x, c)) for d in range(32) for y, x, c in [coords(d)]]


def cross_shift(r, turn):
    both = (y_shift(r), x_shift(r))
    return [both[(d % NC + turn) % 2][d] for d in range(32)]


def xor_perm(n, bit):
    return [(i, i ^ bit) for i in range(n)]


NEAR = [(z, z ^ 1) for z in range(NZ)]
FAR = [(z, (z - 1) % NZ if z % 2 == 0 else (z + 1) % NZ) for z in range(NZ)]


def params(mib=60):
    return pltpu.CompilerParams(vmem_limit_bytes=mib * MIB)


CORE, X, PARITY, SLOT, Y = 8, 9, 10, 11, 15
SUM_ROWS = 16


def shard_body(n_parts, ks, fresh, factor, sc, *refs):
    at = 0
    step = pl.program_id(0)
    values = []
    for n in n_parts:
        if n == 2:
            values.append(jnp.where(step % 2 == 0, refs[at][...], refs[at + 1][...]))
        else:
            values.append(refs[at][...])
        at += n
    og_ref, we_ref = refs[at], refs[at + 1]
    wn_ref, keep_ref, send_ref = refs[at + (2 if fresh else 3) :]
    a = values[0] if len(values) == 1 else jnp.where(step < 2, values[0], values[1])
    partial = lax.dot_general(a, og_ref[...], (((0,), (0,)), ((), ())), preferred_element_type=F32)
    corrected = partial * factor + we_ref[0].astype(F32)
    rows = corrected.shape[0] // 2
    out = []
    for b in range(2):
        block = corrected[b * rows : (b + 1) * rows]
        level = jnp.sum(jnp.abs(block), axis=(0, 1), keepdims=True) * (1.0 / block.size) + 1e-06
        packed = (level * jnp.tanh(block / level)).astype(BF)
        wn_ref[0, b * rows : (b + 1) * rows] = (block - packed.astype(F32)).astype(BF)
        out.append(packed)
    first = sc[CORE] == 0
    keep_ref[0] = jnp.where(first, out[0], out[1])
    send_ref[0] = jnp.where(first, out[1], out[0])


def shard_grad(sc, parts, ks, og, worker_error, wn, factor):
    tokens, cols = og.shape
    wide = worker_error.shape[1] // NZ // 2
    count = 2 * len(parts)
    in_specs, args = [], []
    for k, part in enumerate(parts):
        for piece in part:
            if len(part) == 2:
                in_specs.append(pl.BlockSpec((tokens, wide), lambda g, s: (0, 0)))
            else:
                in_specs.append(
                    pl.BlockSpec(
                        (tokens, wide), lambda g, s, k=k: (0, jnp.clip(g - 2 * k, 0, 1))
                    )
                )
            args.append(piece)

    def error_at(g, s):
        m = s[ks[0]] if len(ks) == 1 else jnp.where(g < 2, s[ks[0]], s[ks[1]])
        return (0, 2 * m + g % 2, 0)

    in_specs += [
        pl.BlockSpec((tokens, cols), lambda g, s: (0, 0)),
        pl.BlockSpec((1, wide, cols), error_at),
    ]
    args += [og, worker_error]
    aliases = {}
    if wn is not None:
        aliases[1 + len(args)] = 0
        args.append(wn)
        in_specs.append(pl.BlockSpec(memory_space=pl.ANY))
    block = pl.BlockSpec((1, wide // 2, cols), lambda g, s: (g, 0, 0))
    half = jax.ShapeDtypeStruct((count, wide // 2, cols), BF)
    return pl.pallas_call(
        functools.partial(shard_body, [len(p) for p in parts], ks, wn is None, factor),
        grid_spec=pltpu.PrefetchScalarGridSpec(
            num_scalar_prefetch=1,
            grid=(count,),
            in_specs=in_specs,
            out_specs=[pl.BlockSpec((1, wide, cols), error_at), block, block],
        ),
        out_shape=[jax.ShapeDtypeStruct(worker_error.shape, BF), half, half],
        input_output_aliases=aliases,
        compiler_params=params(),
        cost_estimate=pl.CostEstimate(
            flops=2 * tokens * count * wide * cols,
            bytes_accessed=6 * count * wide * cols,
            transcendentals=0,
        ),
        name="shard_grad",
    )(sc, *args)


def core_sum_body(n, sc, *refs):
    outs = refs[4 * n :]
    for r in range(NX):
        x = lax.rem(sc[X] + r, NX)
        same = jnp.bitwise_xor(x // 2, sc[PARITY]) == 0
        h = lax.rem(x, 2)
        for p in range(n):
            a, ra, b, rb = refs[4 * p : 4 * p + 4]
            first = a[h].astype(F32) + ra[h].astype(F32)
            second = b[h].astype(F32) + rb[h].astype(F32)
            outs[r][p] = jnp.where(same, first, second).astype(outs[r].dtype)


def core_sum(sc, pairs):
    tail = pairs[0][0][0].shape[1:]
    n = len(pairs)
    args, in_specs = [], []
    for pair in pairs:
        for keep, recv, half in pair:
            args += [keep, recv]
            in_specs += [pl.BlockSpec((2,) + tail, lambda i, s, half=half: (half, 0, 0))] * 2
    one = pl.BlockSpec((n,) + tail, lambda i, s: (0, 0, 0))
    return pl.pallas_call(
        functools.partial(core_sum_body, n),
        grid_spec=pltpu.PrefetchScalarGridSpec(
            num_scalar_prefetch=1, grid=(1,), in_specs=in_specs, out_specs=[one] * 4
        ),
        out_shape=[jax.ShapeDtypeStruct((n,) + tail, F32 if r == 0 else BF) for r in range(NX)],
        compiler_params=params(),
        name="core_sum",
    )(sc, *args)


def x_sum_body(counts, sc, *refs):
    outs, held = refs[-5:-1], refs[-1]
    at, p = 0, 0
    for n in counts:
        for k in range(n):
            held[sc[SLOT + p]] = sum(refs[at + r][k].astype(F32) for r in range(NX))
            p += 1
        at += NX
    for r in range(NY):
        outs[r][...] = held[r].astype(outs[r].dtype)


def x_sum(sc, groups):
    tail = groups[0][0].shape[1:]
    args = [v for group in groups for v in group]
    one = pl.BlockSpec(tail, lambda i, s: (0, 0))
    return pl.pallas_call(
        functools.partial(x_sum_body, [g[0].shape[0] for g in groups]),
        grid_spec=pltpu.PrefetchScalarGridSpec(
            num_scalar_prefetch=1,
            grid=(1,),
            in_specs=[pl.BlockSpec(v.shape, lambda i, s: (0, 0, 0)) for v in args],
            out_specs=[one] * 4,
            scratch_shapes=[pltpu.VMEM((NY,) + tail, F32)],
        ),
        out_shape=[jax.ShapeDtypeStruct(tail, F32 if r == 0 else BF) for r in range(NY)],
        compiler_params=params(8),
        name="x_sum",
    )(sc, *args)


def three_parts(value):
    high = value.astype(BF).astype(F32)
    middle = (value - high).astype(BF).astype(F32)
    return high, middle, value - high - middle


def update_body(sc, g0, g1, g2, g3, w, mom, var, err, mom_out, err_out, stay, leave, held_dir):
    gradient = (
        g0[...] + g1[...].astype(F32) + g2[...].astype(F32) + g3[...].astype(F32)
    )
    momentum = 0.9 * mom[...] + 0.1 * gradient
    mom_out[...] = momentum
    held = momentum + err[...]
    level = jnp.sum(jnp.abs(held), axis=(0, 1), keepdims=True) * (1.0 / held.size) + 1e-06
    squeezed = level * jnp.tanh(held / level)
    err_out[...] = held - squeezed
    direction = (squeezed / (jnp.sqrt(var[...]) + 1e-06)).astype(BF)
    held_dir[...] = direction
    wf = w[...].astype(F32)
    df = direction.astype(F32)
    total_w = jnp.sum(wf * wf, axis=(0, 1), keepdims=True)
    total_d = jnp.sum(df * df, axis=(0, 1), keepdims=True)
    half, cols = direction.shape[0] // 2, direction.shape[1]
    row = lax.broadcasted_iota(jnp.int32, (SUM_ROWS, cols), 0)
    extra = jnp.zeros((SUM_ROWS, cols), F32)
    for k, part in enumerate(three_parts(total_w) + three_parts(total_d)):
        extra = jnp.where(row == k, part, extra)
    for out, which in ((stay, sc[CORE]), (leave, 1 - sc[CORE])):
        out[0:half] = held_dir[pl.ds(pl.multiple_of(which * half, half), half), :]
        out[half:] = extra.astype(BF)


def update(sc, mine, got, weight, momentum, variance, server_error):
    shape = weight.shape
    part = (shape[0] // 2 + SUM_ROWS, shape[1])
    one = pl.BlockSpec(shape, lambda i, s: (0, 0))
    half = pl.BlockSpec(part, lambda i, s: (0, 0))
    return pl.pallas_call(
        update_body,
        grid_spec=pltpu.PrefetchScalarGridSpec(
            num_scalar_prefetch=1,
            grid=(1,),
            in_specs=[one] * 8,
            out_specs=[one, one, half, half],
            scratch_shapes=[pltpu.VMEM(shape, BF)],
        ),
        out_shape=[
            jax.ShapeDtypeStruct(shape, F32),
            jax.ShapeDtypeStruct(shape, F32),
            jax.ShapeDtypeStruct(part, BF),
            jax.ShapeDtypeStruct(part, BF),
        ],
        compiler_params=params(8),
        name="update",
    )(sc, mine, *got, weight, momentum, variance, server_error)


def plane_sums_body(a, b, c, d, out):
    total = sum(jnp.sum(v[...].astype(F32), axis=(0, 1)) for v in (a, b, c, d))
    weights = total[0:1] + total[1:2] + total[2:3]
    directions = total[3:4] + total[4:5] + total[5:6]
    row = lax.broadcasted_iota(jnp.int32, out.shape, 0)
    out[...] = jnp.where(row == 0, weights, directions)


def plane_sums(gathered):
    lead = gathered[0].shape[:2]
    at = gathered[0].shape[2] // SUM_ROWS - 1
    return pl.pallas_call(
        plane_sums_body,
        grid=(1,),
        in_specs=[pl.BlockSpec(lead + (SUM_ROWS, 128), lambda i: (0, 0, at, 0))] * 4,
        out_specs=pl.BlockSpec((8, 128), lambda i: (0, 0)),
        out_shape=jax.ShapeDtypeStruct((8, 128), F32),
        compiler_params=params(8),
        name="plane_sums",
    )(*gathered)


def forward_body(n_parts, ending, sc, *refs):
    n = sum(n_parts)
    pieces = refs[:n]
    out, a_held, b_held, a_sems, b_sems = refs[-5:]
    quarter = b_held.shape[1] // 4
    waits = []
    at = 0
    for k, parts in enumerate(n_parts):
        wide = 4 * quarter // parts
        mine = []
        for j in range(parts):
            target = a_held.at[k] if parts == 1 else a_held.at[k, :, j * wide : (j + 1) * wide]
            mine.append(pltpu.make_async_copy(pieces[at], target, a_sems.at[at]))
            at += 1
        if not ending:
            for i in range(4):
                target = b_held.at[k, i * quarter : (i + 1) * quarter]
                mine.append(pltpu.make_async_copy(refs[n].at[sc[k], i, 0], target, b_sems.at[k]))
        for copy in mine:
            copy.start()
        waits.append(mine)
    if ending:
        half = quarter // 2
        for r2 in range(4):
            for refs_of, core in ((refs[n : n + 4], sc[CORE]), (refs[n + 4 : n + 8], 1 - sc[CORE])):
                for r1 in range(4):
                    x = lax.rem(sc[X] - jnp.where(core == 0, r2, r1) + NX, NX)
                    y = lax.rem(sc[Y] - jnp.where(core == 0, r1, r2) + NY, NY)
                    for other in range(2):
                        block = 2 * lax.rem(x, 2) + (core if other == 0 else 1 - core)
                        row = pl.multiple_of(block * quarter + core * half, half)
                        m = 2 * y + x // 2
                        pltpu.make_async_copy(
                            refs_of[r2].at[r1, other, 0:half],
                            b_held.at[m, pl.ds(row, half)],
                            b_sems.at[m],
                        ).start()
        for k, mine in enumerate(waits):
            m = sc[k]
            for i in range(8):
                target = b_held.at[m, i * half : (i + 1) * half]
                mine.append(pltpu.make_async_copy(refs[n].at[0, 0, 0:half], target, b_sems.at[m]))
    total = None
    for k, mine in enumerate(waits):
        for copy in mine:
            copy.wait()
        part = jnp.dot(a_held[k], b_held[sc[k] if ending else k], preferred_element_type=F32)
        total = part if total is None else total + part
    out[...] = total.astype(out.dtype)


def forward(sc, parts, matrices, ending):
    tokens, rows = parts[0][0].shape
    cols = matrices[0].shape[-1]
    args = [v for part in parts for v in part]
    n = len(args)
    args = args + list(matrices)
    return pl.pallas_call(
        functools.partial(forward_body, [len(p) for p in parts], ending),
        grid_spec=pltpu.PrefetchScalarGridSpec(
            num_scalar_prefetch=1,
            grid=(1,),
            in_specs=[pl.BlockSpec(memory_space=pl.ANY)] * len(args),
            out_specs=pl.BlockSpec((tokens, cols), lambda i, s: (0, 0)),
            scratch_shapes=[
                pltpu.VMEM((NZ, tokens, rows), BF),
                pltpu.VMEM((NZ, rows, cols), BF),
                pltpu.SemaphoreType.DMA((n,)),
                pltpu.SemaphoreType.DMA((NZ,)),
            ],
        ),
        out_shape=jax.ShapeDtypeStruct((tokens, cols), F32),
        compiler_params=params(),
        cost_estimate=pl.CostEstimate(
            flops=2 * NZ * tokens * cols * rows, bytes_accessed=6 * NZ * rows * cols, transcendentals=0
        ),
        name="forward",
    )(sc, *args)


def input_grad_body(sc, og, w, out, acc):
    j = pl.program_id(0)
    wide = jnp.concatenate([w[0, i, 0] for i in range(4)])
    part = lax.dot_general(og[0], wide, (((1,), (1,)), ((), ())), preferred_element_type=F32)

    @pl.when(j == 0)
    def _():
        acc[...] = part

    @pl.when(j > 0)
    def _():
        acc[...] += part

    @pl.when(j == NZ - 1)
    def _():
        out[...] = acc[...].astype(BF)


def input_grad_of(sc, og_all, both):
    _, tokens, cols = og_all.shape
    width = 4 * both.shape[3]
    return pl.pallas_call(
        input_grad_body,
        grid_spec=pltpu.PrefetchScalarGridSpec(
            num_scalar_prefetch=1,
            grid=(NZ,),
            in_specs=[
                pl.BlockSpec((1, tokens, cols), lambda j, s: (lax.rem(j - s[0] + NZ, NZ), 0, 0)),
                pl.BlockSpec((1, 4, 1, width // 4, cols), lambda j, s: (j, 0, 1, 0, 0)),
            ],
            out_specs=pl.BlockSpec((tokens, width), lambda j, s: (0, 0)),
            scratch_shapes=[pltpu.VMEM((tokens, width), F32)],
        ),
        out_shape=jax.ShapeDtypeStruct((tokens, width), BF),
        compiler_params=params(),
        cost_estimate=pl.CostEstimate(
            flops=2 * NZ * tokens * cols * width, bytes_accessed=2 * og_all.size, transcendentals=0
        ),
        name="input_grad",
    )(sc, og_all, both)


def shards(inputs, out_grad, weight, momentum, variance, server_error, worker_error):
    groups = lax.axis_size("dp")
    factor = 1.0 / math.sqrt(inputs.shape[0] * groups)
    rows, cols = weight.shape
    z = lax.axis_index("mp")
    d = lax.axis_index("dp")
    y, x, core = d // (NX * NC), (d // NC) % NX, d % NC
    parity = z % 2
    sign = 1 - 2 * parity
    wide = inputs.shape[1] // 2

    spread_perm, along_perm = [], []
    for dp in range(32):
        yy, xx, cc = coords(dp)
        for zz in range(NZ):
            row = 2 * yy + xx // 2
            place = (row + zz) % NZ
            to = flat_dp(place // 2, 2 * (place % 2) + xx % 2, cc)
            spread_perm.append((dp * NZ + zz, to * NZ + zz))
            along_perm.append((to * NZ + zz, to * NZ + row))

    def near(a):
        return lax.ppermute(a, "mp", NEAR)

    def away(a):
        return lax.ppermute(a, "mp", FAR)

    def at(k):
        return lax.rem(z + k * sign + 2 * NZ, NZ)

    ms = [at(0), at(1), at(-1), at(-2), at(2), at(3), at(-3), at(4)]
    slots = [lax.rem(ms[k] // 2 - y + NY, NY) for k in (0, 3, 4, 7)]
    sc = jnp.stack(ms + [core, x, parity] + slots + [y]).astype(jnp.int32)
    tie = lax.optimization_barrier

    def grad(parts, ks, wn):
        return shard_grad(sc, parts, ks, out_grad, worker_error, wn, factor)

    def swap(send):
        return lax.ppermute(send, "dp", xor_perm(32, 1))

    def spread(mine):
        return [mine[0]] + [lax.ppermute(mine[r], "dp", x_shift(r)) for r in (1, 2, 3)]

    moved = lax.ppermute(weight, ("dp", "mp"), spread_perm)
    moved = lax.ppermute(moved, ("dp", "mp"), along_perm)
    u1, v1 = near(inputs), away(inputs)
    u1, v1, moved = tie((u1, v1, moved))

    both = lax.all_gather(jnp.concatenate([weight, moved]), "dp", axis=0, tiled=True)
    both = both.reshape(NZ, 4, 2, rows, cols)
    u2, v2 = near(v1), away(u1)
    wn, keep0, send0 = grad([(inputs,)], [0], None)
    recv0 = swap(send0)
    wn, keep1, send1 = grad([(u1,), (v1,)], [1, 2], wn)
    recv1 = swap(send1)
    u2, v2, wn, recv0, recv1 = tie((u2, v2, wn, recv0, recv1))

    u3, v3 = near(v2), away(u2)
    wn, keep2, send2 = grad([(v2,), (u2,)], [3, 4], wn)
    recv2 = swap(send2)
    sums01 = core_sum(
        sc,
        [
            ((keep0, recv0, 0), (keep1, recv1, 0)),
            ((keep2, recv2, 0), (keep1, recv1, 1)),
        ],
    )
    u3, v3, wn, sums01 = tie((u3, v3, wn, sums01))

    g0, g1, wn = tie((v3[:, :wide], u3[:, wide:], wn))
    f0, f1 = near(g0), away(g1)
    wn, keep3, send3 = grad([(u3,), (v3,)], [5, 6], wn)
    f0, f1, wn, send3, later = tie((f0, f1, wn, send3, out_grad))

    og_all = lax.all_gather(later, "mp", axis=0, tiled=False)
    blocks01 = spread(sums01)
    recv3 = swap(send3)
    wn, keep4, send4 = grad([(f0, f1)], [7], wn)
    recv4 = swap(send4)
    sums23 = core_sum(
        sc,
        [
            ((keep2, recv2, 1), (keep3, recv3, 0)),
            ((keep4, recv4, 0), (keep3, recv3, 1)),
        ],
    )
    sums23, blocks01 = tie((sums23, blocks01))
    blocks23 = spread(sums23)
    parts = [(inputs,), (u1,), (v1,), (v2,), (u2,), (u3,), (v3,), (f0, f1)]
    base = forward(sc, parts, [both], False)
    blocks23, base = tie((blocks23, base))
    by_y = x_sum(sc, [blocks01, blocks23])
    got = [lax.ppermute(by_y[r], "dp", y_shift(r)) for r in (1, 2, 3)]
    momentum_next, server_next, stay, leave = update(
        sc, by_y[0], got, weight, momentum, variance, server_error
    )
    halves = jnp.stack([stay, swap(leave)])
    line = jnp.stack([halves] + [lax.ppermute(halves, "dp", cross_shift(r, 0)) for r in (1, 2, 3)])
    square = [line] + [lax.ppermute(line, "dp", cross_shift(r, 1)) for r in (1, 2, 3)]
    input_grad = input_grad_of(sc, og_all, both)
    theirs = [swap(line)]
    *square, theirs[0], input_grad = tie((*square, theirs[0], input_grad))
    theirs += [swap(v) for v in square[1:]]
    sums = plane_sums(square)
    sums = sums + lax.ppermute(sums, "mp", xor_perm(NZ, 1))
    *theirs, sums = tie((*theirs, sums))
    others = [lax.ppermute(sums, "mp", xor_perm(NZ, k)) for k in (2, 4, 6)]
    change = forward(sc, parts, square + theirs, True)
    change, *others = tie((change, *others))
    sums = sums + others[0] + others[1] + others[2]
    ratio = jnp.sqrt(sums[0, 0] / (sums[1, 0] + 1e-12))
    refreshed = (base - 0.25 * ratio * change).astype(BF)
    return (input_grad, momentum_next, server_next, wn, refreshed)


def solution(mesh):
    return jax.shard_map(
        shards,
        mesh=mesh,
        in_specs=(
            P("dp", "mp"),
            P("dp", "mp"),
            P("dp", "mp"),
            P("dp", "mp"),
            P("dp", "mp"),
            P("dp", "mp"),
            P("dp", None, "mp"),
        ),
        out_specs=(P("dp", "mp"), P("dp", "mp"), P("dp", "mp"), P("dp", None, "mp"), P("dp", "mp")),
        check_vma=False,
    )
```
